32 devices in a mesh: rep: 8 (over y, x, core), shard: 4 (over z).
Axes of the slice: x: 2, y: 2, z: 4, core: 2. Of those that a mesh axis runs over, the one named last changes fastest.
Arguments:
- tokens: bfloat16 [6144, 768], P(('rep', 'shard')), may hold values from -6 to 6
- seq_len: int32 [8, 8], P('rep'), may hold values from 1 to 672, as said below
- norm_gain: bfloat16 [2, 2, 768], P(None, None, 'shard'), may hold values from 0.5 to 1.5
- norm_bias: bfloat16 [2, 2, 768], P(None, None, 'shard'), may hold values from -1.5 to 1.5
- w_qkv: bfloat16 [2, 768, 2304], P(None, 'shard'), may hold values from -0.21875 to 0.21875
- b_qkv: bfloat16 [2, 2304], P(None, 'shard'), may hold values from -1.5 to 1.5
- w_out: bfloat16 [2, 768, 768], P(None, 'shard'), may hold values from -1.75 to 1.75
- b_out: bfloat16 [2, 768], P(None, 'shard'), may hold values from -1.5 to 1.5
- w_up: bfloat16 [2, 768, 3072], P(None, 'shard'), may hold values from -0.21875 to 0.21875
- b_up: bfloat16 [2, 3072], P(None, 'shard'), may hold values from -1.5 to 1.5
- w_down: bfloat16 [2, 3072, 768], P(None, 'shard'), may hold values from -0.109375 to 0.109375
- b_down: bfloat16 [2, 768], P(None, 'shard'), may hold values from -1.5 to 1.5
- cotangent: float32 [6144, 768], P(('rep', 'shard')), may hold values from -6 to 6
Outputs:
- output: float32 [6144, 768], P(('rep', 'shard'))
- grad_tokens: float32 [6144, 768], P(('rep', 'shard'))
- grad_norm_gain: float32 [2, 2, 768], P(None, None, 'shard')
- grad_norm_bias: float32 [2, 2, 768], P(None, None, 'shard')
- grad_w_qkv: float32 [2, 768, 2304], P(None, 'shard')
- grad_b_qkv: float32 [2, 2304], P(None, 'shard')
- grad_w_out: float32 [2, 768, 768], P(None, 'shard')
- grad_b_out: float32 [2, 768], P(None, 'shard')
- grad_w_up: float32 [2, 768, 3072], P(None, 'shard')
- grad_b_up: float32 [2, 3072], P(None, 'shard')
- grad_w_down: float32 [2, 3072, 768], P(None, 'shard')
- grad_b_down: float32 [2, 768], P(None, 'shard')
The draws below stay inside these ranges and needn't reach their ends.
Inputs may be any that keep to these rules, and one draw needn't show every extreme that they name: `seq_len`: row r holds the lengths of replica group r's 8 sequences in order; they sum to 768; the second is exactly 672 long and the first is at most 48 long.
All inputs are finite; a program needn't handle non-finite values.
Results may differ from the reference program's by a relative error of at most 0.015.
Values may be sent and summed in bfloat16 or wider, within the bound.
A program may use at most 192 MiB of HBM per device.

```python
import math
import jax
import jax.numpy as jnp
from jax import lax

D = 768
HEADS = 12
HEAD = 64
ROT = 16
FF = 3072
LAYERS = 2
NSEQ = 8
TOK_DEV = 192
GROUP = 768
TOKENS = 6144
LONGEST = 672
N_REP = 8
N_SHARD = 4


def draw_seq_len(key, part):
    key = jax.random.fold_in(key, 7)
    head_key, share_key = jax.random.split(key)
    inner = NSEQ - 2
    leading = jax.random.randint(head_key, (N_REP, 1), 1, TOK_DEV // 4 + 1, dtype=jnp.int32)
    remain = GROUP - LONGEST - leading
    shares = jax.random.randint(share_key, (N_REP, inner), 1, 100, dtype=jnp.int32)
    spare = remain - inner
    pieces = 1 + shares * spare // jnp.sum(shares, axis=1, keepdims=True, dtype=jnp.int32)
    closing = remain - jnp.sum(pieces[:, :-1], axis=1, keepdims=True, dtype=jnp.int32)
    longest = jnp.full((N_REP, 1), LONGEST, jnp.int32)
    return jnp.concatenate([leading, longest, pieces[:, :-1], closing], axis=1).astype(jnp.int32)


def block_levels(key, dims, cuts, least, high):
    loudness, own = 1.0, jax.random.fold_in(key, 6)
    for dim, blocks in cuts:
        draws = jnp.exp(jax.random.uniform(jax.random.fold_in(own, dim), (blocks,), jnp.float32, least / len(cuts), high / len(cuts)))
        loudness = loudness * jnp.repeat(draws, dims[dim] // blocks).reshape([-1 if axis == dim else 1 for axis in range(len(dims))])
    return loudness


def scatter_about(key, dims, scale, most, cuts=(), kind=jnp.bfloat16):
    drawn = jax.random.normal(key, dims, jnp.float32) * scale
    if len(cuts) > 0:
        drawn = block_levels(key, dims, cuts, -0.22, 0.18) * drawn
    return jnp.clip(drawn, min=-most, max=most).astype(kind)


def setup_inputs(seed: int = 0) -> dict:
    seeds = jax.random.split(jax.random.key(seed), 14)
    return {
        "tokens": scatter_about(seeds[0], (TOKENS, D), 1.0, 6.0, ((0, 32),)),
        "seq_len": draw_seq_len(jax.random.fold_in(seeds[13], 71), 0),
        "norm_gain": jnp.clip(1.0 + 0.1 * jax.random.normal(seeds[2], (LAYERS, 2, D), jnp.float32), 0.5, 1.5).astype(jnp.bfloat16),
        "norm_bias": scatter_about(seeds[3], (LAYERS, 2, D), 0.3, 1.5, ((2, 4),)),
        "w_qkv": scatter_about(seeds[4], (LAYERS, D, 3 * D), D ** -0.5, 0.21875, ((1, 4),)),
        "b_qkv": scatter_about(seeds[5], (LAYERS, 3 * D), 0.3, 1.5, ((1, 4),)),
        "w_out": scatter_about(seeds[6], (LAYERS, D, D), (D // 64) ** -0.5, 1.75, ((1, 4),)),
        "b_out": scatter_about(seeds[7], (LAYERS, D), 0.3, 1.5, ((1, 4),)),
        "w_up": scatter_about(seeds[8], (LAYERS, D, FF), D ** -0.5, 0.21875, ((1, 4),)),
        "b_up": scatter_about(seeds[9], (LAYERS, FF), 0.3, 1.5, ((1, 4),)),
        "w_down": scatter_about(seeds[10], (LAYERS, FF, D), FF ** -0.5, 0.109375, ((1, 4),)),
        "b_down": scatter_about(seeds[11], (LAYERS, D), 0.3, 1.5, ((1, 4),)),
        "cotangent": scatter_about(seeds[12], (TOKENS, D), 1.0, 6.0, ((0, 32),), jnp.float32),
    }


@jax.custom_vjp
def low(v):
    return lax.optimization_barrier(v.astype(jnp.bfloat16)).astype(jnp.float32)

@jax.custom_vjp
def low_back(v):
    return v

def low_keep(v):
    return (low(v), None)

def low_pass(kept, grad):
    return (grad,)

def back_keep(v):
    return (v, None)

def back_low(kept, grad):
    return (low(grad),)
low.defvjp(low_keep, low_pass)
low_back.defvjp(back_keep, back_low)
EPSILON = 1e-05
HIGHEST = lax.Precision.HIGHEST

def layer_norm(values, gain, shift):
    center = values - lax.optimization_barrier(jnp.mean(values, axis=-1, keepdims=True))
    spread = lax.optimization_barrier(jnp.mean(center * center, axis=-1, keepdims=True))
    return center * lax.rsqrt(spread + EPSILON) * gain + shift

def sequence_layout(lengths, total):
    ends = jnp.cumsum(lengths, dtype=jnp.int32)
    starts = ends - lengths
    offsets = jnp.arange(total, dtype=jnp.int32)
    after = offsets[:, None] >= starts[None, :]
    doc_ids = lax.optimization_barrier(jnp.sum(after.astype(jnp.int32), axis=1, dtype=jnp.int32)) - 1
    begins = lax.optimization_barrier(jnp.max(jnp.where(after, starts[None, :], 0), axis=1)).astype(jnp.int32)
    return (doc_ids, offsets - begins)

def rotary_tables(places):
    inverse = jnp.exp(jnp.arange(ROT // 2, dtype=jnp.float32) * (-2.0 * math.log(10000.0) / ROT))
    angles = places.astype(jnp.float32)[:, None] * inverse[None, :]
    return (jnp.cos(angles), jnp.sin(angles))

def rotate(field, cosine, sine):
    half = ROT // 2
    leading = field[..., :half]
    trailing = field[..., half:ROT]
    cos_rows = cosine[:, None, :]
    sin_rows = sine[:, None, :]
    return jnp.concatenate([leading * cos_rows - trailing * sin_rows, trailing * cos_rows + leading * sin_rows, field[..., ROT:]], axis=-1)

def attention(queries, key_rows, value_rows, doc_ids):
    groups, total = doc_ids.shape
    block_width = math.gcd(total, 512)
    blocks = total // block_width
    score_scale = 1.0 / math.sqrt(HEAD)
    positions = jnp.arange(total, dtype=jnp.int32)

    def one_group(items):
        group_q, group_k, group_v, group_doc = items

        @jax.checkpoint
        def one_block(block_items):
            block_q, block_doc, block_pos = block_items
            scores = jnp.einsum('qhd,khd->hqk', block_q, group_k, precision=HIGHEST) * score_scale
            allowed = (block_doc[:, None] == group_doc[None, :]) & (block_pos[:, None] >= positions[None, :])
            scores = low_back(jnp.where(allowed[None], scores, -1e+30))
            weights = low(jax.nn.softmax(scores, axis=-1))
            return jnp.einsum('hqk,khd->qhd', weights, group_v, precision=HIGHEST)
        result = lax.map(one_block, (group_q.reshape(blocks, block_width, HEADS, HEAD), group_doc.reshape(blocks, block_width), positions.reshape(blocks, block_width)))
        return result.reshape(total, HEADS, HEAD)

    def shaped(array):
        return array.reshape(groups, total, HEADS, HEAD)
    result = lax.map(one_group, (shaped(queries), shaped(key_rows), shaped(value_rows), doc_ids))
    return result.reshape(groups * total, HEADS * HEAD)

def layer(resid, gains, shifts, w_mixed, b_mixed, w_attn, b_attn, w_hidden, b_hidden, w_back, b_back, doc_ids, cosine, sine):
    rows = resid.shape[0]
    normed_one = low(layer_norm(resid, gains[0], shifts[0]))
    normed_two = low(layer_norm(resid, gains[1], shifts[1]))
    mixed = low_back(jnp.dot(normed_one, w_mixed, precision=HIGHEST) + b_mixed)
    queries = low(rotate(mixed[:, :D].reshape(rows, HEADS, HEAD), cosine, sine))
    key_rows = low(rotate(mixed[:, D:2 * D].reshape(rows, HEADS, HEAD), cosine, sine))
    value_rows = low(mixed[:, 2 * D:].reshape(rows, HEADS, HEAD))
    attended = attention(queries, key_rows, value_rows, doc_ids)
    attended = low(low_back(attended))
    branch_attn = low_back(jnp.dot(attended, w_attn, precision=HIGHEST) + b_attn)
    hidden = low_back(jnp.dot(normed_two, w_hidden, precision=HIGHEST) + b_hidden)
    active = low(jax.nn.gelu(hidden, approximate=False))
    branch_mlp = low_back(jnp.dot(active, w_back, precision=HIGHEST) + b_back)
    return resid + branch_attn + branch_mlp

def reference(tokens, seq_len, norm_gain, norm_bias, w_qkv, b_qkv, w_out, b_out, w_up, b_up, w_down, b_down, cotangent):
    group_rows = TOK_DEV * N_SHARD
    doc_ids, places = jax.vmap(lambda lengths: sequence_layout(lengths, group_rows))(seq_len)
    cosine, sine = rotary_tables(places.reshape(-1))
    params = tuple((p.astype(jnp.float32) for p in (norm_gain, norm_bias, w_qkv, b_qkv, w_out, b_out, w_up, b_up, w_down, b_down)))

    def forward(inputs, weights):
        resid = inputs
        for layer_index in range(LAYERS):
            resid = layer(resid, *[member[layer_index] for member in weights], doc_ids, cosine, sine)
        return resid
    output, pullback = jax.vjp(forward, tokens.astype(jnp.float32), params)
    grad_tokens, grads = pullback(cotangent)
    return (output, grad_tokens, grads[0], grads[1], grads[2], grads[3], grads[4], grads[5], grads[6], grads[7], grads[8], grads[9])
```

```python
import math

import jax
import jax.numpy as jnp
from jax import lax
from jax.sharding import PartitionSpec as P

HEADS = 12
HEAD = 64
ROT = 16
LAYERS = 2


EPSILON = 1e-05
MASKED = -1e30


def layer_norm(values, gain, shift):
    center = values - jnp.mean(values, axis=-1, keepdims=True)
    spread = jnp.mean(center * center, axis=-1, keepdims=True)
    return center * lax.rsqrt(spread + EPSILON) * gain + shift


def sequence_layout(lengths, total):
    ends = jnp.cumsum(lengths, dtype=jnp.int32)
    starts = ends - lengths
    offsets = jnp.arange(total, dtype=jnp.int32)
    after = offsets[:, None] >= starts[None, :]
    doc_ids = jnp.sum(after.astype(jnp.int32), axis=1, dtype=jnp.int32) - 1
    begins = jnp.max(jnp.where(after, starts[None, :], 0), axis=1)
    return (doc_ids, offsets - begins)


def rotary_tables(places):
    inverse = jnp.exp(jnp.arange(ROT // 2, dtype=jnp.float32) * (-2.0 * math.log(10000.0) / ROT))
    angles = places.astype(jnp.float32)[:, None] * inverse[None, :]
    return (jnp.cos(angles), jnp.sin(angles))


def rotate(field, cosine, sine):
    half = ROT // 2
    leading = field[..., :half]
    trailing = field[..., half:ROT]
    cos_rows = cosine[:, None, :]
    sin_rows = sine[:, None, :]
    return jnp.concatenate(
        [
            leading * cos_rows - trailing * sin_rows,
            trailing * cos_rows + leading * sin_rows,
            field[..., ROT:],
        ],
        axis=-1,
    )


def score_block(queries, key_block, query_doc, query_pos, key_doc, key_pos, score_scale):
    scores = (
        jnp.einsum("qhd,khd->hqk", queries, key_block, preferred_element_type=jnp.float32)
        * score_scale
    )
    allowed = (query_doc[:, None] == key_doc[None, :]) & (query_pos[:, None] >= key_pos[None, :])
    return jnp.where(allowed[None], scores, MASKED)


def attend_forward(
    queries, key_blocks, value_blocks, query_doc, query_pos, doc_blocks, pos_blocks, score_scale
):
    local_rows = queries.shape[0]
    blocks_in = (key_blocks, value_blocks, doc_blocks, pos_blocks)

    def collect_stats(carry, items):
        running_max, running_sum = carry
        key_block, value_block, key_doc, key_pos = items
        scores = score_block(
            queries, key_block, query_doc, query_pos, key_doc, key_pos, score_scale
        )
        new_max = jnp.maximum(running_max, jnp.max(scores, axis=-1))
        running_sum = running_sum * jnp.exp(running_max - new_max) + jnp.sum(
            jnp.exp(scores - new_max[..., None]), axis=-1
        )
        return ((new_max, running_sum), None)

    start_stats = (
        jnp.full((HEADS, local_rows), MASKED, jnp.float32),
        jnp.zeros((HEADS, local_rows), jnp.float32),
    )
    (top_score, total_sum), _ = lax.scan(collect_stats, start_stats, blocks_in)
    log_total = top_score + jnp.log(total_sum)

    def apply_weights(carry, items):
        rounded_sum, remainder_sum = carry
        key_block, value_block, key_doc, key_pos = items
        scores = score_block(
            queries, key_block, query_doc, query_pos, key_doc, key_pos, score_scale
        )
        weights = jnp.exp(scores - log_total[..., None])
        upper = weights.astype(jnp.bfloat16)
        lower = (weights - upper.astype(jnp.float32)).astype(jnp.bfloat16)
        rounded_sum = rounded_sum + jnp.einsum(
            "hqk,khd->qhd", upper, value_block, preferred_element_type=jnp.float32
        )
        remainder_sum = remainder_sum + jnp.einsum(
            "hqk,khd->qhd", lower, value_block, preferred_element_type=jnp.float32
        )
        return ((rounded_sum, remainder_sum), None)

    zero_out = jnp.zeros(queries.shape, jnp.float32)
    (attended, remainder), _ = lax.scan(apply_weights, (zero_out, zero_out), blocks_in)
    return (attended, log_total, attended + remainder)


def attend_backward(
    queries,
    key_blocks,
    value_blocks,
    grad_out,
    log_total,
    delta,
    query_doc,
    query_pos,
    doc_blocks,
    pos_blocks,
    score_scale,
):

    def step_back(grad_query, items):
        key_block, value_block, key_doc, key_pos = items
        scores = score_block(
            queries, key_block, query_doc, query_pos, key_doc, key_pos, score_scale
        )
        weights = jnp.exp(scores - log_total[..., None])
        grad_weights = jnp.einsum(
            "qhd,khd->hqk", grad_out, value_block, preferred_element_type=jnp.float32
        )
        grad_scores = (weights * (grad_weights - delta[..., None])).astype(jnp.bfloat16)
        grad_query = (
            grad_query
            + jnp.einsum("hqk,khd->qhd", grad_scores, key_block, preferred_element_type=jnp.float32)
            * score_scale
        )
        grad_value = jnp.einsum(
            "hqk,qhd->khd",
            weights.astype(jnp.bfloat16),
            grad_out,
            preferred_element_type=jnp.float32,
        )
        grad_key = (
            jnp.einsum("hqk,qhd->khd", grad_scores, queries, preferred_element_type=jnp.float32)
            * score_scale
        )
        return (grad_query, (grad_key, grad_value))

    grad_query, outputs = lax.scan(
        step_back,
        jnp.zeros(queries.shape, jnp.float32),
        (key_blocks, value_blocks, doc_blocks, pos_blocks),
    )
    return (grad_query, outputs[0].reshape(-1, HEADS * HEAD), outputs[1].reshape(-1, HEADS * HEAD))


def gathered_per_device(
    tokens,
    seq_len,
    norm_gain,
    norm_bias,
    w_qkv,
    b_qkv,
    w_out,
    b_out,
    w_up,
    b_up,
    w_down,
    b_down,
    cotangent,
):
    shards = lax.axis_size("shard")
    device_rank = lax.axis_index("shard")
    local_rows = tokens.shape[0]
    model_width = w_out.shape[2]
    group_rows = local_rows * shards
    doc_ids, places = sequence_layout(seq_len[0], group_rows)
    group_pos = jnp.arange(group_rows, dtype=jnp.int32)
    first_row = device_rank * local_rows
    query_doc = lax.dynamic_slice_in_dim(doc_ids, first_row, local_rows)
    query_pos = lax.dynamic_slice_in_dim(group_pos, first_row, local_rows)
    query_place = lax.dynamic_slice_in_dim(places, first_row, local_rows)
    cosine, sine = rotary_tables(query_place)
    factor = 1
    while factor * local_rows < 512 and shards % (factor * 2) == 0:
        factor = factor * 2
    block_rows = factor * local_rows
    block_count = group_rows // block_rows
    doc_blocks = doc_ids.reshape(block_count, block_rows)
    pos_blocks = group_pos.reshape(block_count, block_rows)
    score_scale = 1.0 / math.sqrt(HEAD)

    def as_blocks(array):
        return array.reshape(block_count, block_rows, HEADS, HEAD)

    resid = tokens.astype(jnp.float32)
    stored = []
    for layer_index in range(LAYERS):
        params = (
            lax.all_gather(norm_gain[layer_index], "shard", axis=1, tiled=True),
            lax.all_gather(norm_bias[layer_index], "shard", axis=1, tiled=True),
            lax.all_gather(w_qkv[layer_index], "shard", axis=0, tiled=True),
            lax.all_gather(b_qkv[layer_index], "shard", axis=0, tiled=True),
            lax.all_gather(w_out[layer_index], "shard", axis=0, tiled=True),
            lax.all_gather(b_out[layer_index], "shard", axis=0, tiled=True),
            lax.all_gather(w_up[layer_index], "shard", axis=0, tiled=True),
            lax.all_gather(b_up[layer_index], "shard", axis=0, tiled=True),
            lax.all_gather(w_down[layer_index], "shard", axis=0, tiled=True),
            lax.all_gather(b_down[layer_index], "shard", axis=0, tiled=True),
        )
        (
            gains,
            shifts,
            weight_qkv,
            bias_qkv,
            weight_out,
            bias_out,
            weight_up,
            bias_up,
            weight_down,
            bias_down,
        ) = params
        normed_one = layer_norm(
            resid, gains[0].astype(jnp.float32), shifts[0].astype(jnp.float32)
        ).astype(jnp.bfloat16)
        normed_two = layer_norm(
            resid, gains[1].astype(jnp.float32), shifts[1].astype(jnp.float32)
        ).astype(jnp.bfloat16)
        mixed = jnp.dot(
            normed_one, weight_qkv, preferred_element_type=jnp.float32
        ) + bias_qkv.astype(jnp.float32)
        queries = rotate(
            mixed[:, :model_width].reshape(local_rows, HEADS, HEAD), cosine, sine
        ).astype(jnp.bfloat16)
        key_rows = (
            rotate(
                mixed[:, model_width : 2 * model_width].reshape(local_rows, HEADS, HEAD),
                cosine,
                sine,
            )
            .astype(jnp.bfloat16)
            .reshape(local_rows, model_width)
        )
        value_rows = mixed[:, 2 * model_width :].astype(jnp.bfloat16)
        key_all, value_all = (
            lax.all_gather(key_rows, "shard", axis=0, tiled=True),
            lax.all_gather(value_rows, "shard", axis=0, tiled=True),
        )
        attended, log_total, exact_out = attend_forward(
            queries,
            as_blocks(key_all),
            as_blocks(value_all),
            query_doc,
            query_pos,
            doc_blocks,
            pos_blocks,
            score_scale,
        )
        attended16 = attended.reshape(local_rows, model_width).astype(jnp.bfloat16)
        branch_attn = jnp.dot(
            attended16, weight_out, preferred_element_type=jnp.float32
        ) + bias_out.astype(jnp.float32)
        hidden = jnp.dot(
            normed_two, weight_up, preferred_element_type=jnp.float32
        ) + bias_up.astype(jnp.float32)
        active16 = jax.nn.gelu(hidden, approximate=False).astype(jnp.bfloat16)
        branch_mlp = jnp.dot(
            active16, weight_down, preferred_element_type=jnp.float32
        ) + bias_down.astype(jnp.float32)
        stored.append(
            (
                resid,
                normed_one,
                normed_two,
                queries,
                key_rows,
                value_rows,
                key_all,
                value_all,
                attended16,
                log_total,
                exact_out,
                hidden,
                active16,
                params,
            )
        )
        resid = resid + branch_attn + branch_mlp
    gradient = cotangent
    layer_grads = []
    for layer_index in range(LAYERS - 1, -1, -1):
        (
            resid_in,
            normed_one,
            normed_two,
            queries,
            key_rows,
            value_rows,
            key_all,
            value_all,
            attended16,
            log_total,
            exact_out,
            hidden,
            active16,
            params,
        ) = stored[layer_index]
        weights = (
            lax.all_gather(norm_gain[layer_index], "shard", axis=1, tiled=True),
            lax.all_gather(norm_bias[layer_index], "shard", axis=1, tiled=True),
            lax.all_gather(w_qkv[layer_index], "shard", axis=0, tiled=True),
            lax.all_gather(b_qkv[layer_index], "shard", axis=0, tiled=True),
            lax.all_gather(w_out[layer_index], "shard", axis=0, tiled=True),
            lax.all_gather(b_out[layer_index], "shard", axis=0, tiled=True),
            lax.all_gather(w_up[layer_index], "shard", axis=0, tiled=True),
            lax.all_gather(b_up[layer_index], "shard", axis=0, tiled=True),
            lax.all_gather(w_down[layer_index], "shard", axis=0, tiled=True),
            lax.all_gather(b_down[layer_index], "shard", axis=0, tiled=True),
        )
        key_again, value_again = (
            lax.all_gather(key_rows, "shard", axis=0, tiled=True),
            lax.all_gather(value_rows, "shard", axis=0, tiled=True),
        )
        (
            gains,
            shifts,
            weight_qkv,
            bias_qkv,
            weight_out,
            bias_out,
            weight_up,
            bias_up,
            weight_down,
            bias_down,
        ) = weights
        grad16 = gradient.astype(jnp.bfloat16)
        grad_bias_sum = jnp.sum(grad16, axis=0, dtype=jnp.float32)
        grad_w_attn = jnp.dot(attended16.T, grad16, preferred_element_type=jnp.float32)
        grad_w_back = jnp.dot(active16.T, grad16, preferred_element_type=jnp.float32)
        grad_attended = (
            jnp.dot(grad16, weight_out.T, preferred_element_type=jnp.float32)
            .astype(jnp.bfloat16)
            .reshape(local_rows, HEADS, HEAD)
        )
        grad_active = jnp.dot(grad16, weight_down.T, preferred_element_type=jnp.float32)
        _, gelu_pull = jax.vjp(lambda values: jax.nn.gelu(values, approximate=False), hidden)
        grad_hidden = gelu_pull(grad_active)[0].astype(jnp.bfloat16)
        grad_w_hidden = jnp.dot(normed_two.T, grad_hidden, preferred_element_type=jnp.float32)
        grad_b_hidden = jnp.sum(grad_hidden, axis=0, dtype=jnp.float32)
        grad_second = jnp.dot(grad_hidden, weight_up.T, preferred_element_type=jnp.float32)
        delta = jnp.sum(grad_attended.astype(jnp.float32) * exact_out, axis=-1).T
        grad_query, grad_keys_all, grad_values_all = attend_backward(
            queries,
            as_blocks(key_again),
            as_blocks(value_again),
            grad_attended,
            log_total,
            delta,
            query_doc,
            query_pos,
            doc_blocks,
            pos_blocks,
            score_scale,
        )
        grad_keys, grad_values = (
            lax.psum_scatter(
                grad_keys_all.astype(jnp.bfloat16), "shard", scatter_dimension=0, tiled=True
            ).astype(jnp.float32),
            lax.psum_scatter(
                grad_values_all.astype(jnp.bfloat16), "shard", scatter_dimension=0, tiled=True
            ).astype(jnp.float32),
        )
        grad_query_pre = rotate(grad_query, cosine, -sine).reshape(local_rows, model_width)
        grad_keys_pre = rotate(grad_keys.reshape(local_rows, HEADS, HEAD), cosine, -sine).reshape(
            local_rows, model_width
        )
        grad_mixed = jnp.concatenate([grad_query_pre, grad_keys_pre, grad_values], axis=1).astype(
            jnp.bfloat16
        )
        grad_w_mixed = jnp.dot(normed_one.T, grad_mixed, preferred_element_type=jnp.float32)
        grad_b_mixed = jnp.sum(grad_mixed, axis=0, dtype=jnp.float32)
        grad_first = jnp.dot(grad_mixed, weight_qkv.T, preferred_element_type=jnp.float32)
        _, pull_one = jax.vjp(
            layer_norm, resid_in, gains[0].astype(jnp.float32), shifts[0].astype(jnp.float32)
        )
        _, pull_two = jax.vjp(
            layer_norm, resid_in, gains[1].astype(jnp.float32), shifts[1].astype(jnp.float32)
        )
        back_one = pull_one(grad_first)
        back_two = pull_two(grad_second)
        grad_gains = jnp.stack([back_one[1], back_two[1]])
        grad_shifts = jnp.stack([back_one[2], back_two[2]])
        gradient = gradient + back_one[0] + back_two[0]
        reduced = (
            lax.psum_scatter(
                grad_gains.astype(jnp.bfloat16), "shard", scatter_dimension=1, tiled=True
            ).astype(jnp.float32),
            lax.psum_scatter(
                grad_shifts.astype(jnp.bfloat16), "shard", scatter_dimension=1, tiled=True
            ).astype(jnp.float32),
            lax.psum_scatter(
                grad_w_mixed.astype(jnp.bfloat16), "shard", scatter_dimension=0, tiled=True
            ).astype(jnp.float32),
            lax.psum_scatter(
                grad_b_mixed.astype(jnp.bfloat16), "shard", scatter_dimension=0, tiled=True
            ).astype(jnp.float32),
            lax.psum_scatter(
                grad_w_attn.astype(jnp.bfloat16), "shard", scatter_dimension=0, tiled=True
            ).astype(jnp.float32),
            lax.psum_scatter(
                grad_bias_sum.astype(jnp.bfloat16), "shard", scatter_dimension=0, tiled=True
            ).astype(jnp.float32),
            lax.psum_scatter(
                grad_w_hidden.astype(jnp.bfloat16), "shard", scatter_dimension=0, tiled=True
            ).astype(jnp.float32),
            lax.psum_scatter(
                grad_b_hidden.astype(jnp.bfloat16), "shard", scatter_dimension=0, tiled=True
            ).astype(jnp.float32),
            lax.psum_scatter(
                grad_w_back.astype(jnp.bfloat16), "shard", scatter_dimension=0, tiled=True
            ).astype(jnp.float32),
            lax.psum_scatter(
                grad_bias_sum.astype(jnp.bfloat16), "shard", scatter_dimension=0, tiled=True
            ).astype(jnp.float32),
        )
        reduced = (
            lax.psum(reduced[0].astype(jnp.bfloat16), "rep").astype(jnp.float32),
            lax.psum(reduced[1].astype(jnp.bfloat16), "rep").astype(jnp.float32),
            lax.psum(reduced[2].astype(jnp.bfloat16), "rep").astype(jnp.float32),
            lax.psum(reduced[3].astype(jnp.bfloat16), "rep").astype(jnp.float32),
            lax.psum(reduced[4].astype(jnp.bfloat16), "rep").astype(jnp.float32),
            lax.psum(reduced[5].astype(jnp.bfloat16), "rep").astype(jnp.float32),
            lax.psum(reduced[6].astype(jnp.bfloat16), "rep").astype(jnp.float32),
            lax.psum(reduced[7].astype(jnp.bfloat16), "rep").astype(jnp.float32),
            lax.psum(reduced[8].astype(jnp.bfloat16), "rep").astype(jnp.float32),
            lax.psum(reduced[9].astype(jnp.bfloat16), "rep").astype(jnp.float32),
        )
        layer_grads.append(reduced)
    layer_grads = layer_grads[::-1]
    stacked = [
        jnp.stack([layer_grads[layer_pos][member] for layer_pos in range(LAYERS)])
        for member in range(10)
    ]
    return (
        resid,
        gradient,
        stacked[0],
        stacked[1],
        stacked[2],
        stacked[3],
        stacked[4],
        stacked[5],
        stacked[6],
        stacked[7],
        stacked[8],
        stacked[9],
    )


def by_heads(array):
    heads = array.shape[1] // HEAD
    return jnp.stack([array[:, h * HEAD : (h + 1) * HEAD] for h in range(heads)])


def from_heads(array):
    return jnp.concatenate([array[h] for h in range(array.shape[0])], axis=1)


def rotary_lanes(places, width):
    half = ROT // 2
    lane = jnp.arange(width, dtype=jnp.int32) % HEAD
    inverse = jnp.exp((lane % half).astype(jnp.float32) * (-2.0 * math.log(10000.0) / ROT))
    angles = places.astype(jnp.float32)[:, None] * inverse[None, :]
    cosine, sine = jnp.cos(angles), jnp.sin(angles)
    keep = jnp.where(lane < ROT, cosine, 1.0)
    from_right = jnp.where(lane < half, -sine, 0.0)
    from_left = jnp.where((lane >= half) & (lane < ROT), sine, 0.0)
    return (keep, from_right, from_left)


def rotate_lanes(field, tables, sign):
    half = ROT // 2
    keep, from_right, from_left = tables
    turned = jnp.roll(field, -half, axis=1) * from_right + jnp.roll(field, half, axis=1) * from_left
    return field * keep + sign * turned


def dot32(left, right):
    return jnp.dot(left, right, preferred_element_type=jnp.float32)


def normalize(rows):
    center = rows - jnp.mean(rows, axis=-1, keepdims=True)
    scale = lax.rsqrt(jnp.mean(center * center, axis=-1, keepdims=True) + EPSILON)
    return (center * scale, scale)


def norm_back(grad, unit, scale):
    level = jnp.mean(grad, axis=-1, keepdims=True)
    along = jnp.mean(grad * unit, axis=-1, keepdims=True)
    return scale * (grad - level - unit * along)


def split_per_device(
    tokens,
    seq_len,
    norm_gain,
    norm_bias,
    w_qkv,
    b_qkv,
    w_out,
    b_out,
    w_up,
    b_up,
    w_down,
    b_down,
    cotangent,
):
    shards = lax.axis_size("shard")
    rank = lax.axis_index("shard")
    rows, width = tokens.shape
    part = width // shards
    units = w_up.shape[2] // shards
    total = rows * shards
    f32 = jnp.float32
    bf16 = jnp.bfloat16
    score_scale = 1.0 / math.sqrt(HEAD)

    tokens_all = lax.all_gather(tokens, "shard", axis=0, tiled=True)
    small = [norm_gain, norm_bias, b_qkv, b_out, b_down]
    packed = lax.all_gather(jnp.concatenate([v.reshape(-1) for v in small]), "shard", axis=0)
    whole = []
    at = 0
    for v in small:
        piece = packed[:, at : at + v.size].reshape((shards,) + v.shape)
        whole.append(jnp.moveaxis(piece, 0, -2).reshape(v.shape[:-1] + (-1,)).astype(f32))
        at += v.size
    gains, shifts, bias_qkv, bias_out, bias_down = whole
    bias_qkv = lax.dynamic_slice_in_dim(
        bias_qkv.reshape(LAYERS, 3, width), rank * part, part, axis=2
    ).reshape(LAYERS, 3 * part)
    bias_up = b_up.astype(f32)

    columns = []
    for l in range(LAYERS):
        up = w_up[l].reshape(part, shards, units).transpose(1, 0, 2)
        qkv = w_qkv[l].reshape(part, 3, shards, part).transpose(2, 0, 1, 3)
        both = jnp.concatenate([up, qkv.reshape(shards, part, 3 * part)], axis=2)
        both = lax.all_to_all(both, "shard", 0, 0).reshape(width, units + 3 * part)
        columns.append((both[:, :units], both[:, units:]))
    cotangent_all = lax.all_gather(cotangent, "shard", axis=0, tiled=True)

    doc_ids, places = sequence_layout(seq_len[0], total)
    tables = rotary_lanes(places, 2 * part)
    order = jnp.arange(total, dtype=jnp.int32)
    allowed = (doc_ids[:, None] == doc_ids[None, :]) & (order[:, None] >= order[None, :])

    resid = tokens_all.astype(f32)
    stored = []
    output = None
    for l in range(LAYERS):
        col_up, col_qkv = columns[l]
        unit, scale = normalize(resid)
        first = (unit * gains[l, 0] + shifts[l, 0]).astype(bf16)
        second = (unit * gains[l, 1] + shifts[l, 1]).astype(bf16)
        mixed = dot32(first, col_qkv) + bias_qkv[l]
        turned = rotate_lanes(mixed[:, : 2 * part], tables, 1.0).astype(bf16)
        query, key = by_heads(turned[:, :part]), by_heads(turned[:, part:])
        value = by_heads(mixed[:, 2 * part :].astype(bf16))
        scores = jnp.einsum("hqd,hkd->hqk", query, key, preferred_element_type=f32) * score_scale
        scores = jnp.where(allowed[None], scores, MASKED)
        raised = jnp.exp(scores - jnp.max(scores, axis=-1, keepdims=True))
        probs = raised / jnp.sum(raised, axis=-1, keepdims=True)
        probs16 = probs.astype(bf16)
        attended = from_heads(
            jnp.einsum("hqk,hkd->hqd", probs16, value, preferred_element_type=f32).astype(bf16)
        )
        hidden = dot32(second, col_up) + bias_up[l]
        active = jax.nn.gelu(hidden, approximate=False).astype(bf16)
        branch = (dot32(attended, w_out[l]) + dot32(active, w_down[l])).astype(bf16)
        bias = bias_out[l] + bias_down[l]
        stored.append((unit, scale, first, second, query, key, value, probs, attended, hidden, active))
        if l < LAYERS - 1:
            resid = resid + lax.psum(branch, "shard").astype(f32) + bias
        else:
            own = lax.dynamic_slice_in_dim(resid, rank * rows, rows)
            summed = lax.psum_scatter(branch, "shard", scatter_dimension=0, tiled=True)
            output = own + summed.astype(f32) + bias

    gradient = cotangent_all
    grad_tokens = None
    weight_grads = [None] * LAYERS
    vectors = [None] * LAYERS
    for l in range(LAYERS - 1, -1, -1):
        unit, scale, first, second, query, key, value, probs, attended, hidden, active = stored[l]
        col_up, col_qkv = columns[l]
        grad16 = gradient.astype(bf16)
        grad_bias = jnp.sum(grad16, axis=0, dtype=f32)
        grad_down = dot32(active.T, grad16).astype(bf16)
        grad_out = dot32(attended.T, grad16).astype(bf16)
        grad_active = dot32(grad16, w_down[l].T)
        _, pull = jax.vjp(lambda v: jax.nn.gelu(v, approximate=False), hidden)
        grad_hidden = pull(grad_active)[0].astype(bf16)
        grad_up = dot32(second.T, grad_hidden).astype(bf16)
        grad_b_up = jnp.sum(grad_hidden, axis=0, dtype=f32)
        back_second = dot32(grad_hidden, col_up.T)

        grad_att = by_heads(dot32(grad16, w_out[l].T).astype(bf16))
        grad_probs = jnp.einsum("hqd,hkd->hqk", grad_att, value, preferred_element_type=f32)
        delta = jnp.sum(probs * grad_probs, axis=-1, keepdims=True)
        grad_scores = (probs * (grad_probs - delta)).astype(bf16)
        grad_query = jnp.einsum("hqk,hkd->hqd", grad_scores, key, preferred_element_type=f32)
        grad_key = jnp.einsum("hqk,hqd->hkd", grad_scores, query, preferred_element_type=f32)
        grad_value = jnp.einsum(
            "hqk,hqd->hkd", probs.astype(bf16), grad_att, preferred_element_type=f32
        )
        turned = jnp.concatenate([from_heads(grad_query), from_heads(grad_key)], axis=1)
        turned = rotate_lanes(turned * score_scale, tables, -1.0)
        grad_mixed = jnp.concatenate([turned, from_heads(grad_value)], axis=1).astype(bf16)
        grad_b_mixed = jnp.sum(grad_mixed, axis=0, dtype=f32)
        grad_qkv = dot32(first.T, grad_mixed).astype(bf16)
        back_first = dot32(grad_mixed, col_qkv.T)

        combined = (back_first * gains[l, 0] + back_second * gains[l, 1]).astype(bf16)
        if l > 0:
            summed = lax.psum(combined, "shard").astype(f32)
            gradient = gradient + norm_back(summed, unit, scale)
        else:
            summed = lax.psum_scatter(combined, "shard", scatter_dimension=0, tiled=True)
            own = [
                lax.dynamic_slice_in_dim(v, rank * rows, rows) for v in (gradient, unit, scale)
            ]
            grad_tokens = own[0] + norm_back(summed.astype(f32), own[1], own[2])

        moved = jnp.concatenate([grad_up, grad_qkv], axis=1)
        moved = lax.all_to_all(moved.reshape(shards, part, units + 3 * part), "shard", 0, 0)
        weight_grads[l] = lax.psum((moved, grad_out, grad_down), "rep")

        def placed(vector, start, size):
            return lax.dynamic_update_slice_in_dim(jnp.zeros((size,), f32), vector, start, 0)

        own_bias = lax.dynamic_slice_in_dim(grad_bias, rank * part, part)
        vectors[l] = jnp.concatenate(
            [
                jnp.sum(back_first * unit, axis=0),
                jnp.sum(back_second * unit, axis=0),
                jnp.sum(back_first, axis=0),
                jnp.sum(back_second, axis=0),
                *[
                    placed(grad_b_mixed[i * part : (i + 1) * part], rank * part, width)
                    for i in range(3)
                ],
                placed(own_bias, rank * part, width),
                placed(grad_b_up, rank * units, units * shards),
            ]
        )

    small_grads = lax.psum(jnp.stack(vectors), ("rep", "shard"))
    norm_grads = lax.dynamic_slice_in_dim(
        small_grads[:, : 4 * width].reshape(LAYERS, 2, 2, width), rank * part, part, axis=3
    )
    g_b_qkv = lax.dynamic_slice_in_dim(
        small_grads[:, 4 * width : 7 * width], rank * 3 * part, 3 * part, axis=1
    )
    g_b_out = lax.dynamic_slice_in_dim(
        small_grads[:, 7 * width : 8 * width], rank * part, part, axis=1
    )
    g_b_up = lax.dynamic_slice_in_dim(small_grads[:, 8 * width :], rank * units, units, axis=1)

    g_qkv, g_up, g_out, g_down = [], [], [], []
    for l in range(LAYERS):
        moved, grad_out, grad_down = weight_grads[l]
        g_up.append(moved[:, :, :units].transpose(1, 0, 2).reshape(part, -1).astype(f32))
        qkv = moved[:, :, units:].reshape(shards, part, 3, part)
        g_qkv.append(qkv.transpose(1, 2, 0, 3).reshape(part, -1).astype(f32))
        g_out.append(grad_out.astype(f32))
        g_down.append(grad_down.astype(f32))
    return (
        output,
        grad_tokens,
        norm_grads[:, 0],
        norm_grads[:, 1],
        jnp.stack(g_qkv),
        g_b_qkv,
        jnp.stack(g_out),
        g_b_out,
        jnp.stack(g_up),
        g_b_up,
        jnp.stack(g_down),
        g_b_out,
    )


def per_device(*args):
    if HEADS % lax.axis_size("shard") == 0:
        return split_per_device(*args)
    return gathered_per_device(*args)


def solution(mesh):
    return jax.shard_map(
        per_device,
        mesh=mesh,
        in_specs=(
            P(("rep", "shard"), None),
            P("rep", None),
            P(None, None, "shard"),
            P(None, None, "shard"),
            P(None, "shard", None),
            P(None, "shard"),
            P(None, "shard", None),
            P(None, "shard"),
            P(None, "shard", None),
            P(None, "shard"),
            P(None, "shard", None),
            P(None, "shard"),
            P(("rep", "shard"), None),
        ),
        out_specs=(
            P(("rep", "shard"), None),
            P(("rep", "shard"), None),
            P(None, None, "shard"),
            P(None, None, "shard"),
            P(None, "shard", None),
            P(None, "shard"),
            P(None, "shard", None),
            P(None, "shard"),
            P(None, "shard", None),
            P(None, "shard"),
            P(None, "shard", None),
            P(None, "shard"),
        ),
        check_vma=False,
    )
```

```python
import math

import jax
import jax.numpy as jnp
from jax import lax
from jax.sharding import PartitionSpec as P

HEADS = 12
HEAD = 64
ROT = 16
LAYERS = 2


EPSILON = 1e-05
MASKED = -1e30


def layer_norm(values, gain, shift):
    center = values - jnp.mean(values, axis=-1, keepdims=True)
    spread = jnp.mean(center * center, axis=-1, keepdims=True)
    return center * lax.rsqrt(spread + EPSILON) * gain + shift


def sequence_layout(lengths, total):
    ends = jnp.cumsum(lengths, dtype=jnp.int32)
    starts = ends - lengths
    offsets = jnp.arange(total, dtype=jnp.int32)
    after = offsets[:, None] >= starts[None, :]
    doc_ids = jnp.sum(after.astype(jnp.int32), axis=1, dtype=jnp.int32) - 1
    begins = jnp.max(jnp.where(after, starts[None, :], 0), axis=1)
    return (doc_ids, offsets - begins)


def rotary_tables(places):
    inverse = jnp.exp(jnp.arange(ROT // 2, dtype=jnp.float32) * (-2.0 * math.log(10000.0) / ROT))
    angles = places.astype(jnp.float32)[:, None] * inverse[None, :]
    return (jnp.cos(angles), jnp.sin(angles))


def rotate(field, cosine, sine):
    half = ROT // 2
    leading = field[..., :half]
    trailing = field[..., half:ROT]
    cos_rows = cosine[:, None, :]
    sin_rows = sine[:, None, :]
    return jnp.concatenate(
        [
            leading * cos_rows - trailing * sin_rows,
            trailing * cos_rows + leading * sin_rows,
            field[..., ROT:],
        ],
        axis=-1,
    )


def score_block(queries, key_block, query_doc, query_pos, key_doc, key_pos, score_scale):
    scores = (
        jnp.einsum("qhd,khd->hqk", queries, key_block, preferred_element_type=jnp.float32)
        * score_scale
    )
    allowed = (query_doc[:, None] == key_doc[None, :]) & (query_pos[:, None] >= key_pos[None, :])
    return jnp.where(allowed[None], scores, MASKED)


def attend_forward(
    queries, key_blocks, value_blocks, query_doc, query_pos, doc_blocks, pos_blocks, score_scale
):
    local_rows = queries.shape[0]
    blocks_in = (key_blocks, value_blocks, doc_blocks, pos_blocks)

    def collect_stats(carry, items):
        running_max, running_sum = carry
        key_block, value_block, key_doc, key_pos = items
        scores = score_block(
            queries, key_block, query_doc, query_pos, key_doc, key_pos, score_scale
        )
        new_max = jnp.maximum(running_max, jnp.max(scores, axis=-1))
        running_sum = running_sum * jnp.exp(running_max - new_max) + jnp.sum(
            jnp.exp(scores - new_max[..., None]), axis=-1
        )
        return ((new_max, running_sum), None)

    start_stats = (
        jnp.full((HEADS, local_rows), MASKED, jnp.float32),
        jnp.zeros((HEADS, local_rows), jnp.float32),
    )
    (top_score, total_sum), _ = lax.scan(collect_stats, start_stats, blocks_in)
    log_total = top_score + jnp.log(total_sum)

    def apply_weights(carry, items):
        rounded_sum, remainder_sum = carry
        key_block, value_block, key_doc, key_pos = items
        scores = score_block(
            queries, key_block, query_doc, query_pos, key_doc, key_pos, score_scale
        )
        weights = jnp.exp(scores - log_total[..., None])
        upper = weights.astype(jnp.bfloat16)
        lower = (weights - upper.astype(jnp.float32)).astype(jnp.bfloat16)
        rounded_sum = rounded_sum + jnp.einsum(
            "hqk,khd->qhd", upper, value_block, preferred_element_type=jnp.float32
        )
        remainder_sum = remainder_sum + jnp.einsum(
            "hqk,khd->qhd", lower, value_block, preferred_element_type=jnp.float32
        )
        return ((rounded_sum, remainder_sum), None)

    zero_out = jnp.zeros(queries.shape, jnp.float32)
    (attended, remainder), _ = lax.scan(apply_weights, (zero_out, zero_out), blocks_in)
    return (attended, log_total, attended + remainder)


def attend_backward(
    queries,
    key_blocks,
    value_blocks,
    grad_out,
    log_total,
    delta,
    query_doc,
    query_pos,
    doc_blocks,
    pos_blocks,
    score_scale,
):

    def step_back(grad_query, items):
        key_block, value_block, key_doc, key_pos = items
        scores = score_block(
            queries, key_block, query_doc, query_pos, key_doc, key_pos, score_scale
        )
        weights = jnp.exp(scores - log_total[..., None])
        grad_weights = jnp.einsum(
            "qhd,khd->hqk", grad_out, value_block, preferred_element_type=jnp.float32
        )
        grad_scores = (weights * (grad_weights - delta[..., None])).astype(jnp.bfloat16)
        grad_query = (
            grad_query
            + jnp.einsum("hqk,khd->qhd", grad_scores, key_block, preferred_element_type=jnp.float32)
            * score_scale
        )
        grad_value = jnp.einsum(
            "hqk,qhd->khd",
            weights.astype(jnp.bfloat16),
            grad_out,
            preferred_element_type=jnp.float32,
        )
        grad_key = (
            jnp.einsum("hqk,qhd->khd", grad_scores, queries, preferred_element_type=jnp.float32)
            * score_scale
        )
        return (grad_query, (grad_key, grad_value))

    grad_query, outputs = lax.scan(
        step_back,
        jnp.zeros(queries.shape, jnp.float32),
        (key_blocks, value_blocks, doc_blocks, pos_blocks),
    )
    return (grad_query, outputs[0].reshape(-1, HEADS * HEAD), outputs[1].reshape(-1, HEADS * HEAD))


def gathered_per_device(
    tokens,
    seq_len,
    norm_gain,
    norm_bias,
    w_qkv,
    b_qkv,
    w_out,
    b_out,
    w_up,
    b_up,
    w_down,
    b_down,
    cotangent,
):
    shards = lax.axis_size("shard")
    device_rank = lax.axis_index("shard")
    local_rows = tokens.shape[0]
    model_width = w_out.shape[2]
    group_rows = local_rows * shards
    doc_ids, places = sequence_layout(seq_len[0], group_rows)
    group_pos = jnp.arange(group_rows, dtype=jnp.int32)
    first_row = device_rank * local_rows
    query_doc = lax.dynamic_slice_in_dim(doc_ids, first_row, local_rows)
    query_pos = lax.dynamic_slice_in_dim(group_pos, first_row, local_rows)
    query_place = lax.dynamic_slice_in_dim(places, first_row, local_rows)
    cosine, sine = rotary_tables(query_place)
    factor = 1
    while factor * local_rows < 512 and shards % (factor * 2) == 0:
        factor = factor * 2
    block_rows = factor * local_rows
    block_count = group_rows // block_rows
    doc_blocks = doc_ids.reshape(block_count, block_rows)
    pos_blocks = group_pos.reshape(block_count, block_rows)
    score_scale = 1.0 / math.sqrt(HEAD)

    def as_blocks(array):
        return array.reshape(block_count, block_rows, HEADS, HEAD)

    resid = tokens.astype(jnp.float32)
    stored = []
    for layer_index in range(LAYERS):
        params = (
            lax.all_gather(norm_gain[layer_index], "shard", axis=1, tiled=True),
            lax.all_gather(norm_bias[layer_index], "shard", axis=1, tiled=True),
            lax.all_gather(w_qkv[layer_index], "shard", axis=0, tiled=True),
            lax.all_gather(b_qkv[layer_index], "shard", axis=0, tiled=True),
            lax.all_gather(w_out[layer_index], "shard", axis=0, tiled=True),
            lax.all_gather(b_out[layer_index], "shard", axis=0, tiled=True),
            lax.all_gather(w_up[layer_index], "shard", axis=0, tiled=True),
            lax.all_gather(b_up[layer_index], "shard", axis=0, tiled=True),
            lax.all_gather(w_down[layer_index], "shard", axis=0, tiled=True),
            lax.all_gather(b_down[layer_index], "shard", axis=0, tiled=True),
        )
        (
            gains,
            shifts,
            weight_qkv,
            bias_qkv,
            weight_out,
            bias_out,
            weight_up,
            bias_up,
            weight_down,
            bias_down,
        ) = params
        normed_one = layer_norm(
            resid, gains[0].astype(jnp.float32), shifts[0].astype(jnp.float32)
        ).astype(jnp.bfloat16)
        normed_two = layer_norm(
            resid, gains[1].astype(jnp.float32), shifts[1].astype(jnp.float32)
        ).astype(jnp.bfloat16)
        mixed = jnp.dot(
            normed_one, weight_qkv, preferred_element_type=jnp.float32
        ) + bias_qkv.astype(jnp.float32)
        queries = rotate(
            mixed[:, :model_width].reshape(local_rows, HEADS, HEAD), cosine, sine
        ).astype(jnp.bfloat16)
        key_rows = (
            rotate(
                mixed[:, model_width : 2 * model_width].reshape(local_rows, HEADS, HEAD),
                cosine,
                sine,
            )
            .astype(jnp.bfloat16)
            .reshape(local_rows, model_width)
        )
        value_rows = mixed[:, 2 * model_width :].astype(jnp.bfloat16)
        key_all, value_all = (
            lax.all_gather(key_rows, "shard", axis=0, tiled=True),
            lax.all_gather(value_rows, "shard", axis=0, tiled=True),
        )
        attended, log_total, exact_out = attend_forward(
            queries,
            as_blocks(key_all),
            as_blocks(value_all),
            query_doc,
            query_pos,
            doc_blocks,
            pos_blocks,
            score_scale,
        )
        attended16 = attended.reshape(local_rows, model_width).astype(jnp.bfloat16)
        branch_attn = jnp.dot(
            attended16, weight_out, preferred_element_type=jnp.float32
        ) + bias_out.astype(jnp.float32)
        hidden = jnp.dot(
            normed_two, weight_up, preferred_element_type=jnp.float32
        ) + bias_up.astype(jnp.float32)
        active16 = jax.nn.gelu(hidden, approximate=False).astype(jnp.bfloat16)
        branch_mlp = jnp.dot(
            active16, weight_down, preferred_element_type=jnp.float32
        ) + bias_down.astype(jnp.float32)
        stored.append(
            (
                resid,
                normed_one,
                normed_two,
                queries,
                key_rows,
                value_rows,
                key_all,
                value_all,
                attended16,
                log_total,
                exact_out,
                hidden,
                active16,
                params,
            )
        )
        resid = resid + branch_attn + branch_mlp
    gradient = cotangent
    layer_grads = []
    for layer_index in range(LAYERS - 1, -1, -1):
        (
            resid_in,
            normed_one,
            normed_two,
            queries,
            key_rows,
            value_rows,
            key_all,
            value_all,
            attended16,
            log_total,
            exact_out,
            hidden,
            active16,
            params,
        ) = stored[layer_index]
        weights = (
            lax.all_gather(norm_gain[layer_index], "shard", axis=1, tiled=True),
            lax.all_gather(norm_bias[layer_index], "shard", axis=1, tiled=True),
            lax.all_gather(w_qkv[layer_index], "shard", axis=0, tiled=True),
            lax.all_gather(b_qkv[layer_index], "shard", axis=0, tiled=True),
            lax.all_gather(w_out[layer_index], "shard", axis=0, tiled=True),
            lax.all_gather(b_out[layer_index], "shard", axis=0, tiled=True),
            lax.all_gather(w_up[layer_index], "shard", axis=0, tiled=True),
            lax.all_gather(b_up[layer_index], "shard", axis=0, tiled=True),
            lax.all_gather(w_down[layer_index], "shard", axis=0, tiled=True),
            lax.all_gather(b_down[layer_index], "shard", axis=0, tiled=True),
        )
        key_again, value_again = (
            lax.all_gather(key_rows, "shard", axis=0, tiled=True),
            lax.all_gather(value_rows, "shard", axis=0, tiled=True),
        )
        (
            gains,
            shifts,
            weight_qkv,
            bias_qkv,
            weight_out,
            bias_out,
            weight_up,
            bias_up,
            weight_down,
            bias_down,
        ) = weights
        grad16 = gradient.astype(jnp.bfloat16)
        grad_bias_sum = jnp.sum(grad16, axis=0, dtype=jnp.float32)
        grad_w_attn = jnp.dot(attended16.T, grad16, preferred_element_type=jnp.float32)
        grad_w_back = jnp.dot(active16.T, grad16, preferred_element_type=jnp.float32)
        grad_attended = (
            jnp.dot(grad16, weight_out.T, preferred_element_type=jnp.float32)
            .astype(jnp.bfloat16)
            .reshape(local_rows, HEADS, HEAD)
        )
        grad_active = jnp.dot(grad16, weight_down.T, preferred_element_type=jnp.float32)
        _, gelu_pull = jax.vjp(lambda values: jax.nn.gelu(values, approximate=False), hidden)
        grad_hidden = gelu_pull(grad_active)[0].astype(jnp.bfloat16)
        grad_w_hidden = jnp.dot(normed_two.T, grad_hidden, preferred_element_type=jnp.float32)
        grad_b_hidden = jnp.sum(grad_hidden, axis=0, dtype=jnp.float32)
        grad_second = jnp.dot(grad_hidden, weight_up.T, preferred_element_type=jnp.float32)
        delta = jnp.sum(grad_attended.astype(jnp.float32) * exact_out, axis=-1).T
        grad_query, grad_keys_all, grad_values_all = attend_backward(
            queries,
            as_blocks(key_again),
            as_blocks(value_again),
            grad_attended,
            log_total,
            delta,
            query_doc,
            query_pos,
            doc_blocks,
            pos_blocks,
            score_scale,
        )
        grad_keys, grad_values = (
            lax.psum_scatter(
                grad_keys_all.astype(jnp.bfloat16), "shard", scatter_dimension=0, tiled=True
            ).astype(jnp.float32),
            lax.psum_scatter(
                grad_values_all.astype(jnp.bfloat16), "shard", scatter_dimension=0, tiled=True
            ).astype(jnp.float32),
        )
        grad_query_pre = rotate(grad_query, cosine, -sine).reshape(local_rows, model_width)
        grad_keys_pre = rotate(grad_keys.reshape(local_rows, HEADS, HEAD), cosine, -sine).reshape(
            local_rows, model_width
        )
        grad_mixed = jnp.concatenate([grad_query_pre, grad_keys_pre, grad_values], axis=1).astype(
            jnp.bfloat16
        )
        grad_w_mixed = jnp.dot(normed_one.T, grad_mixed, preferred_element_type=jnp.float32)
        grad_b_mixed = jnp.sum(grad_mixed, axis=0, dtype=jnp.float32)
        grad_first = jnp.dot(grad_mixed, weight_qkv.T, preferred_element_type=jnp.float32)
        _, pull_one = jax.vjp(
            layer_norm, resid_in, gains[0].astype(jnp.float32), shifts[0].astype(jnp.float32)
        )
        _, pull_two = jax.vjp(
            layer_norm, resid_in, gains[1].astype(jnp.float32), shifts[1].astype(jnp.float32)
        )
        back_one = pull_one(grad_first)
        back_two = pull_two(grad_second)
        grad_gains = jnp.stack([back_one[1], back_two[1]])
        grad_shifts = jnp.stack([back_one[2], back_two[2]])
        gradient = gradient + back_one[0] + back_two[0]
        reduced = (
            lax.psum_scatter(
                grad_gains.astype(jnp.bfloat16), "shard", scatter_dimension=1, tiled=True
            ).astype(jnp.float32),
            lax.psum_scatter(
                grad_shifts.astype(jnp.bfloat16), "shard", scatter_dimension=1, tiled=True
            ).astype(jnp.float32),
            lax.psum_scatter(
                grad_w_mixed.astype(jnp.bfloat16), "shard", scatter_dimension=0, tiled=True
            ).astype(jnp.float32),
            lax.psum_scatter(
                grad_b_mixed.astype(jnp.bfloat16), "shard", scatter_dimension=0, tiled=True
            ).astype(jnp.float32),
            lax.psum_scatter(
                grad_w_attn.astype(jnp.bfloat16), "shard", scatter_dimension=0, tiled=True
            ).astype(jnp.float32),
            lax.psum_scatter(
                grad_bias_sum.astype(jnp.bfloat16), "shard", scatter_dimension=0, tiled=True
            ).astype(jnp.float32),
            lax.psum_scatter(
                grad_w_hidden.astype(jnp.bfloat16), "shard", scatter_dimension=0, tiled=True
            ).astype(jnp.float32),
            lax.psum_scatter(
                grad_b_hidden.astype(jnp.bfloat16), "shard", scatter_dimension=0, tiled=True
            ).astype(jnp.float32),
            lax.psum_scatter(
                grad_w_back.astype(jnp.bfloat16), "shard", scatter_dimension=0, tiled=True
            ).astype(jnp.float32),
            lax.psum_scatter(
                grad_bias_sum.astype(jnp.bfloat16), "shard", scatter_dimension=0, tiled=True
            ).astype(jnp.float32),
        )
        reduced = (
            lax.psum(reduced[0].astype(jnp.bfloat16), "rep").astype(jnp.float32),
            lax.psum(reduced[1].astype(jnp.bfloat16), "rep").astype(jnp.float32),
            lax.psum(reduced[2].astype(jnp.bfloat16), "rep").astype(jnp.float32),
            lax.psum(reduced[3].astype(jnp.bfloat16), "rep").astype(jnp.float32),
            lax.psum(reduced[4].astype(jnp.bfloat16), "rep").astype(jnp.float32),
            lax.psum(reduced[5].astype(jnp.bfloat16), "rep").astype(jnp.float32),
            lax.psum(reduced[6].astype(jnp.bfloat16), "rep").astype(jnp.float32),
            lax.psum(reduced[7].astype(jnp.bfloat16), "rep").astype(jnp.float32),
            lax.psum(reduced[8].astype(jnp.bfloat16), "rep").astype(jnp.float32),
            lax.psum(reduced[9].astype(jnp.bfloat16), "rep").astype(jnp.float32),
        )
        layer_grads.append(reduced)
    layer_grads = layer_grads[::-1]
    stacked = [
        jnp.stack([layer_grads[layer_pos][member] for layer_pos in range(LAYERS)])
        for member in range(10)
    ]
    return (
        resid,
        gradient,
        stacked[0],
        stacked[1],
        stacked[2],
        stacked[3],
        stacked[4],
        stacked[5],
        stacked[6],
        stacked[7],
        stacked[8],
        stacked[9],
    )


def by_heads(array):
    heads = array.shape[1] // HEAD
    return jnp.stack([array[:, h * HEAD : (h + 1) * HEAD] for h in range(heads)])


def from_heads(array):
    return jnp.concatenate([array[h] for h in range(array.shape[0])], axis=1)


def rotary_lanes(places, width):
    half = ROT // 2
    lane = jnp.arange(width, dtype=jnp.int32) % HEAD
    inverse = jnp.exp((lane % half).astype(jnp.float32) * (-2.0 * math.log(10000.0) / ROT))
    angles = places.astype(jnp.float32)[:, None] * inverse[None, :]
    cosine, sine = jnp.cos(angles), jnp.sin(angles)
    keep = jnp.where(lane < ROT, cosine, 1.0)
    from_right = jnp.where(lane < half, -sine, 0.0)
    from_left = jnp.where((lane >= half) & (lane < ROT), sine, 0.0)
    return (keep, from_right, from_left)


def rotate_lanes(field, tables, sign):
    half = ROT // 2
    keep, from_right, from_left = tables
    turned = jnp.roll(field, -half, axis=1) * from_right + jnp.roll(field, half, axis=1) * from_left
    return field * keep + sign * turned


def dot32(left, right):
    return jnp.dot(left, right, preferred_element_type=jnp.float32)


def normalize(rows):
    center = rows - jnp.mean(rows, axis=-1, keepdims=True)
    scale = lax.rsqrt(jnp.mean(center * center, axis=-1, keepdims=True) + EPSILON)
    return (center * scale, scale)


def norm_back(grad, unit, scale):
    level = jnp.mean(grad, axis=-1, keepdims=True)
    along = jnp.mean(grad * unit, axis=-1, keepdims=True)
    return scale * (grad - level - unit * along)


def split_per_device(
    tokens,
    seq_len,
    norm_gain,
    norm_bias,
    w_qkv,
    b_qkv,
    w_out,
    b_out,
    w_up,
    b_up,
    w_down,
    b_down,
    cotangent,
):
    shards = lax.axis_size("shard")
    rank = lax.axis_index("shard")
    rows, width = tokens.shape
    part = width // shards
    units = w_up.shape[2] // shards
    total = rows * shards
    f32 = jnp.float32
    bf16 = jnp.bfloat16
    score_scale = 1.0 / math.sqrt(HEAD)

    tokens_all = lax.all_gather(tokens, "shard", axis=0, tiled=True)
    small = [norm_gain, norm_bias, b_qkv, b_out, b_down]
    packed = lax.all_gather(jnp.concatenate([v.reshape(-1) for v in small]), "shard", axis=0)
    whole = []
    at = 0
    for v in small:
        piece = packed[:, at : at + v.size].reshape((shards,) + v.shape)
        whole.append(jnp.moveaxis(piece, 0, -2).reshape(v.shape[:-1] + (-1,)).astype(f32))
        at += v.size
    gains, shifts, bias_qkv, bias_out, bias_down = whole
    bias_qkv = lax.dynamic_slice_in_dim(
        bias_qkv.reshape(LAYERS, 3, width), rank * part, part, axis=2
    ).reshape(LAYERS, 3 * part)
    bias_up = b_up.astype(f32)

    columns = []
    for l in range(LAYERS):
        up = w_up[l].reshape(part, shards, units).transpose(1, 0, 2)
        qkv = w_qkv[l].reshape(part, 3, shards, part).transpose(2, 0, 1, 3)
        both = jnp.concatenate([up, qkv.reshape(shards, part, 3 * part)], axis=2)
        both = lax.all_to_all(both, "shard", 0, 0).reshape(width, units + 3 * part)
        columns.append((both[:, :units], both[:, units:]))
    cotangent_all = None

    doc_ids, places = sequence_layout(seq_len[0], total)
    tables = rotary_lanes(places, 2 * part)
    order = jnp.arange(total, dtype=jnp.int32)
    allowed = (doc_ids[:, None] == doc_ids[None, :]) & (order[:, None] >= order[None, :])

    resid = tokens_all.astype(f32)
    stored = []
    output = None
    for l in range(LAYERS):
        col_up, col_qkv = columns[l]
        unit, scale = normalize(resid)
        first = (unit * gains[l, 0] + shifts[l, 0]).astype(bf16)
        second = (unit * gains[l, 1] + shifts[l, 1]).astype(bf16)
        if l == 0:
            late, first = lax.optimization_barrier((cotangent.astype(bf16), first))
            cotangent_all = lax.all_gather(late, "shard", axis=0, tiled=True).astype(f32)
        mixed = dot32(first, col_qkv) + bias_qkv[l]
        turned = rotate_lanes(mixed[:, : 2 * part], tables, 1.0).astype(bf16)
        query, key = by_heads(turned[:, :part]), by_heads(turned[:, part:])
        value = by_heads(mixed[:, 2 * part :].astype(bf16))
        scores = jnp.einsum("hqd,hkd->hqk", query, key, preferred_element_type=f32) * score_scale
        scores = jnp.where(allowed[None], scores, MASKED)
        raised = jnp.exp(scores - jnp.max(scores, axis=-1, keepdims=True))
        probs = raised / jnp.sum(raised, axis=-1, keepdims=True)
        probs16 = probs.astype(bf16)
        attended = from_heads(
            jnp.einsum("hqk,hkd->hqd", probs16, value, preferred_element_type=f32).astype(bf16)
        )
        hidden = dot32(second, col_up) + bias_up[l]
        active = jax.nn.gelu(hidden, approximate=False).astype(bf16)
        branch = (dot32(attended, w_out[l]) + dot32(active, w_down[l])).astype(bf16)
        bias = bias_out[l] + bias_down[l]
        stored.append((unit, scale, first, second, query, key, value, probs, attended, hidden, active))
        if l < LAYERS - 1:
            resid = resid + lax.psum(branch, "shard").astype(f32) + bias
        else:
            own = lax.dynamic_slice_in_dim(resid, rank * rows, rows)
            summed = lax.psum_scatter(branch, "shard", scatter_dimension=0, tiled=True)
            output = own + summed.astype(f32) + bias

    gradient = cotangent_all
    own_gradient = cotangent
    grad_tokens = None
    weight_grads = [None] * LAYERS
    vectors = [None] * LAYERS
    for l in range(LAYERS - 1, -1, -1):
        unit, scale, first, second, query, key, value, probs, attended, hidden, active = stored[l]
        col_up, col_qkv = columns[l]
        grad16 = gradient.astype(bf16)
        grad_bias = jnp.sum(grad16, axis=0, dtype=f32)
        grad_down = dot32(active.T, grad16).astype(bf16)
        grad_out = dot32(attended.T, grad16).astype(bf16)
        grad_active = dot32(grad16, w_down[l].T)
        _, pull = jax.vjp(lambda v: jax.nn.gelu(v, approximate=False), hidden)
        grad_hidden = pull(grad_active)[0].astype(bf16)
        grad_up = dot32(second.T, grad_hidden).astype(bf16)
        grad_b_up = jnp.sum(grad_hidden, axis=0, dtype=f32)
        back_second = dot32(grad_hidden, col_up.T)

        grad_att = by_heads(dot32(grad16, w_out[l].T).astype(bf16))
        grad_probs = jnp.einsum("hqd,hkd->hqk", grad_att, value, preferred_element_type=f32)
        delta = jnp.sum(probs * grad_probs, axis=-1, keepdims=True)
        grad_scores = (probs * (grad_probs - delta)).astype(bf16)
        grad_query = jnp.einsum("hqk,hkd->hqd", grad_scores, key, preferred_element_type=f32)
        grad_key = jnp.einsum("hqk,hqd->hkd", grad_scores, query, preferred_element_type=f32)
        grad_value = jnp.einsum(
            "hqk,hqd->hkd", probs.astype(bf16), grad_att, preferred_element_type=f32
        )
        turned = jnp.concatenate([from_heads(grad_query), from_heads(grad_key)], axis=1)
        turned = rotate_lanes(turned * score_scale, tables, -1.0)
        grad_mixed = jnp.concatenate([turned, from_heads(grad_value)], axis=1).astype(bf16)
        grad_b_mixed = jnp.sum(grad_mixed, axis=0, dtype=f32)
        grad_qkv = dot32(first.T, grad_mixed).astype(bf16)
        back_first = dot32(grad_mixed, col_qkv.T)

        combined = (back_first * gains[l, 0] + back_second * gains[l, 1]).astype(bf16)
        if l > 0:
            summed = lax.psum(combined, "shard").astype(f32)
            change = norm_back(summed, unit, scale)
            gradient = gradient + change
            own_gradient = own_gradient + lax.dynamic_slice_in_dim(change, rank * rows, rows)
        else:
            summed = lax.psum_scatter(combined, "shard", scatter_dimension=0, tiled=True)
            own = [lax.dynamic_slice_in_dim(v, rank * rows, rows) for v in (unit, scale)]
            grad_tokens = own_gradient + norm_back(summed.astype(f32), own[0], own[1])

        moved = jnp.concatenate([grad_up, grad_qkv], axis=1)
        moved = moved.reshape(shards, part, units + 3 * part)
        if l > 0:
            moved, grad_out, grad_down = lax.psum((moved, grad_out, grad_down), "rep")
            moved = lax.all_to_all(moved, "shard", 0, 0)
            weight_grads[l] = (moved, grad_out, grad_down)
        else:
            moved = lax.all_to_all(moved, "shard", 0, 0)
            weight_grads[l] = lax.psum((moved, grad_out, grad_down), "rep")

        def placed(vector, start, size):
            return lax.dynamic_update_slice_in_dim(jnp.zeros((size,), f32), vector, start, 0)

        own_bias = lax.dynamic_slice_in_dim(grad_bias, rank * part, part)
        vectors[l] = jnp.concatenate(
            [
                jnp.sum(back_first * unit, axis=0),
                jnp.sum(back_second * unit, axis=0),
                jnp.sum(back_first, axis=0),
                jnp.sum(back_second, axis=0),
                *[
                    placed(grad_b_mixed[i * part : (i + 1) * part], rank * part, width)
                    for i in range(3)
                ],
                placed(own_bias, rank * part, width),
                placed(grad_b_up, rank * units, units * shards),
            ]
        )

    small_grads = lax.psum(jnp.stack(vectors), ("rep", "shard"))
    norm_grads = lax.dynamic_slice_in_dim(
        small_grads[:, : 4 * width].reshape(LAYERS, 2, 2, width), rank * part, part, axis=3
    )
    g_b_qkv = lax.dynamic_slice_in_dim(
        small_grads[:, 4 * width : 7 * width], rank * 3 * part, 3 * part, axis=1
    )
    g_b_out = lax.dynamic_slice_in_dim(
        small_grads[:, 7 * width : 8 * width], rank * part, part, axis=1
    )
    g_b_up = lax.dynamic_slice_in_dim(small_grads[:, 8 * width :], rank * units, units, axis=1)

    g_qkv, g_up, g_out, g_down = [], [], [], []
    for l in range(LAYERS):
        moved, grad_out, grad_down = weight_grads[l]
        g_up.append(moved[:, :, :units].transpose(1, 0, 2).reshape(part, -1).astype(f32))
        qkv = moved[:, :, units:].reshape(shards, part, 3, part)
        g_qkv.append(qkv.transpose(1, 2, 0, 3).reshape(part, -1).astype(f32))
        g_out.append(grad_out.astype(f32))
        g_down.append(grad_down.astype(f32))
    return (
        output,
        grad_tokens,
        norm_grads[:, 0],
        norm_grads[:, 1],
        jnp.stack(g_qkv),
        g_b_qkv,
        jnp.stack(g_out),
        g_b_out,
        jnp.stack(g_up),
        g_b_up,
        jnp.stack(g_down),
        g_b_out,
    )


def per_device(*args):
    if HEADS % lax.axis_size("shard") == 0:
        return split_per_device(*args)
    return gathered_per_device(*args)


def solution(mesh):
    return jax.shard_map(
        per_device,
        mesh=mesh,
        in_specs=(
            P(("rep", "shard"), None),
            P("rep", None),
            P(None, None, "shard"),
            P(None, None, "shard"),
            P(None, "shard", None),
            P(None, "shard"),
            P(None, "shard", None),
            P(None, "shard"),
            P(None, "shard", None),
            P(None, "shard"),
            P(None, "shard", None),
            P(None, "shard"),
            P(("rep", "shard"), None),
        ),
        out_specs=(
            P(("rep", "shard"), None),
            P(("rep", "shard"), None),
            P(None, None, "shard"),
            P(None, None, "shard"),
            P(None, "shard", None),
            P(None, "shard"),
            P(None, "shard", None),
            P(None, "shard"),
            P(None, "shard", None),
            P(None, "shard"),
            P(None, "shard", None),
            P(None, "shard"),
        ),
        check_vma=False,
    )
```
